32 devices in a mesh: dp: 8 (over z, x), seq: 4 (over y, core).
Axes of the slice: x: 2, y: 2, z: 4, core: 2. Of those that a mesh axis runs over, the one named last changes fastest.
Arguments:
- tokens: bfloat16 [8, 1024, 1536], P('dp', 'seq'), may hold values from -6 to 6
- modulation: float32 [8, 3, 1536], P('dp'), may hold values from -4 to 4
- heights: int32 [8], P('dp'), may hold values from 16 to 64, as said below
- w_in: bfloat16 [1536, 6144], replicated, may hold values from -0.15625 to 0.15625
- w_x: bfloat16 [3072, 128], replicated, may hold values from -0.109375 to 0.109375
- w_dt: bfloat16 [3072, 96], replicated, may hold values from -0.625 to 0.625
- b_dt: float32 [3072], replicated, may hold values from -7 to -2.5
- a_log: float32 [3072, 16], replicated, may hold values from -1.5 to 1
- d_skip: float32 [3072], replicated, may hold values from 0.5 to 1.5
- conv_w: float32 [3072, 4], replicated, may hold values from -3 to 3
- conv_b: float32 [3072], replicated, may hold values from -0.5 to 0.5
- w_out: bfloat16 [3072, 1536], replicated, may hold values from -0.109375 to 0.109375
- cotangent: bfloat16 [8, 1024, 1536], P('dp', 'seq'), may hold values from -6 to 6
Outputs:
- result: bfloat16 [8, 1024, 1536], P('dp', 'seq')
- grad_tokens: float32 [8, 1024, 1536], P('dp', 'seq')
- grad_w_in: float32 [1536, 6144], P('seq')
- grad_w_x: float32 [3072, 128], P('seq')
- grad_w_dt: float32 [3072, 96], P('seq')
- grad_b_dt: float32 [3072], P('seq')
- grad_a_log: float32 [3072, 16], P('seq')
- grad_d_skip: float32 [3072], P('seq')
- grad_conv_w: float32 [3072, 4], P('seq')
- grad_conv_b: float32 [3072], P('seq')
- grad_w_out: float32 [3072, 1536], P('seq')
The draws below stay inside these ranges and needn't reach their ends.
Inputs may be any that keep to these rules, and one draw needn't show every extreme that they name: `heights`: each height is 16, 32 or 64; the grid's width is 1024 divided by its height.
All inputs are finite; a program needn't handle non-finite values.
Results may differ from the reference program's by a relative error of at most 0.008.
The reference program's roundings to bfloat16 on the way count: a program that leaves them out, or rounds other values in their place, can miss the bound.
Values may be sent and summed in bfloat16 or wider, within the bound.
No kernel may reach another device: no remote copies, remote signals or barrier semaphores. Data moves between devices by JAX's collectives and lax.ppermute only.
A program may use at most 320 MiB of HBM per device.

```python
import jax
import jax.numpy as jnp
from jax import lax

D = 1536
E = 3072
N = 16
R = 96
K = 4
SIDE = 32
BLOCK = 16
GRID_TOK = 1024
ITEMS = 8


def draw_heights(key, part):
    key = jax.random.fold_in(key, 11)
    picks = jax.random.randint(key, (ITEMS,), 0, 3)
    picks = picks.at[0].set(0).at[1].set(2)
    table = jnp.array([1, 2, 4], dtype=jnp.int32)
    return SIDE // 2 * table[picks]


def block_levels(key, extent, split, least, high):
    factor_of, own = 1.0, jax.random.fold_in(key, 6)
    for dim, blocks in split:
        steps = jnp.exp(jax.random.uniform(jax.random.fold_in(own, dim), (blocks,), jnp.float32, least / len(split), high / len(split)))
        factor_of = factor_of * jnp.repeat(steps, extent[dim] // blocks).reshape([-1 if axis == dim else 1 for axis in range(len(extent))])
    return factor_of


def normal_values(own_key, dims, deviation, limit, cuts=(), kind=jnp.bfloat16):
    values = deviation * jax.random.normal(own_key, dims, jnp.float32)
    if cuts:
        values = values * block_levels(own_key, dims, cuts, -0.22, 0.18)
    return jnp.clip(values, -limit, limit).astype(kind)


def setup_inputs(seed: int = 0) -> dict:
    arg_keys = jax.random.split(jax.random.key(seed), 14)
    return {
        "tokens": normal_values(arg_keys[0], (ITEMS, GRID_TOK, D), 1.0, 6.0, ((0, 8), (1, 4))),
        "modulation": normal_values(arg_keys[1], (ITEMS, 3, D), 1.0, 4.0, ((0, 8),), jnp.float32),
        "heights": draw_heights(jax.random.fold_in(arg_keys[13], 71), 0),
        "w_in": normal_values(arg_keys[3], (D, 2 * E), D ** -0.5, 0.15625),
        "w_x": normal_values(arg_keys[4], (E, R + 2 * N), E ** -0.5, 0.109375),
        "w_dt": normal_values(arg_keys[5], (E, R), R ** -0.5, 0.625),
        "b_dt": jnp.clip(jax.random.uniform(arg_keys[6], (E,), jnp.float32, -7.0, -2.5), -7.0, -2.5),
        "a_log": jnp.clip(jax.random.uniform(arg_keys[7], (E, N), jnp.float32, -1.5, 1.0), -1.5, 1.0),
        "d_skip": jnp.clip(jax.random.uniform(arg_keys[8], (E,), jnp.float32, 0.5, 1.5), 0.5, 1.5),
        "conv_w": normal_values(arg_keys[9], (E, K), K ** -0.5, 3.0, (), jnp.float32),
        "conv_b": jnp.clip(jax.random.uniform(arg_keys[10], (E,), jnp.float32, -0.5, 0.5), -0.5, 0.5),
        "w_out": normal_values(arg_keys[11], (E, D), E ** -0.5, 0.109375),
        "cotangent": normal_values(arg_keys[12], (ITEMS, GRID_TOK, D), 1.0, 6.0, ((0, 8), (1, 4))),
    }


epsilon = 1e-06

@jax.custom_vjp
def low(v):
    return lax.optimization_barrier(v.astype(jnp.bfloat16)).astype(jnp.float32)

@jax.custom_vjp
def low_back(v):
    return v

def low_keep(v):
    return (low(v), None)

def low_pass(kept, grad):
    return (grad,)

def back_keep(v):
    return (v, None)

def back_low(kept, grad):
    return (low(grad),)
low.defvjp(low_keep, low_pass)
low_back.defvjp(back_keep, back_low)

def scan_sequence(delta, b_mat, c_mat, inputs, a_mat):
    total = delta.shape[0]
    turns = total // BLOCK

    def step_block(carried, pieces):
        d_part, b_part, c_part, v_part = pieces
        outputs = []
        for position in range(BLOCK):
            decay = jnp.exp(d_part[position][:, None] * a_mat)
            carried = decay * carried + (d_part[position] * v_part[position])[:, None] * b_part[position][None, :]
            outputs.append(lax.optimization_barrier(jnp.sum(carried * c_part[position][None, :], axis=1)))
        return (carried, jnp.stack(outputs))
    pieces = tuple((member.reshape(turns, BLOCK, member.shape[-1]) for member in (delta, b_mat, c_mat, inputs)))
    start = jnp.zeros(a_mat.shape, jnp.float32)
    _, outputs = lax.scan(jax.checkpoint(step_block), start, pieces)
    return outputs.reshape(total, a_mat.shape[0])

def one_direction(proj, inputs, w_dt, b_dt, a_mat):
    low_rank = w_dt.shape[1]
    state_size = a_mat.shape[1]
    pre_delta = jnp.dot(proj[:, :low_rank], w_dt.T, precision=lax.Precision.HIGHEST) + b_dt
    delta = jax.nn.softplus(pre_delta)
    return scan_sequence(delta, proj[:, low_rank:low_rank + state_size], proj[:, low_rank + state_size:], inputs, a_mat)

def item_forward(x_item, mod_item, height, w_in, w_x, w_dt, b_dt, a_mat, d_skip, conv_w, conv_b, w_out):
    highest = lax.Precision.HIGHEST
    total = x_item.shape[0]
    inner_width = w_out.shape[0]
    conv_taps = conv_w.shape[1]
    mean = lax.optimization_barrier(jnp.mean(x_item, axis=-1, keepdims=True))
    centered = x_item - mean
    variance = lax.optimization_barrier(jnp.mean(centered * centered, axis=-1, keepdims=True))
    hmod = low(centered * lax.rsqrt(variance + epsilon) * (1.0 + mod_item[1]) + mod_item[0])
    xz = low_back(jnp.dot(hmod, w_in, precision=highest))
    x_conv = low(xz[:, :inner_width])
    z_gate = xz[:, inner_width:]
    padded = jnp.concatenate([jnp.zeros((conv_taps - 1, inner_width), jnp.float32), x_conv], axis=0)
    pre_conv = conv_b + sum((padded[offset:offset + total] * conv_w[:, offset] for offset in range(conv_taps)))
    u_val = low(jax.nn.silu(pre_conv))
    proj = low(low_back(jnp.dot(u_val, w_x, precision=highest)))
    y_fwd = one_direction(proj, u_val, w_dt, b_dt, a_mat)
    width_of = total // height
    position = jnp.arange(total, dtype=jnp.int32)
    column_pos = total - 1 - position
    order = column_pos % height * width_of + column_pos // height
    u_cols = low_back(u_val)[order]
    proj_cols = low_back(proj)[order]
    y_cols = one_direction(proj_cols, u_cols, w_dt, b_dt, a_mat)
    back = total - 1 - (position % width_of * height + position // width_of)
    y_bwd = low_back(low(y_cols[back]))
    y_all = y_fwd + y_bwd + d_skip * u_val
    gated = low(y_all * jax.nn.silu(z_gate))
    branch = low_back(jnp.dot(gated, w_out, precision=highest))
    return x_item + mod_item[2] * branch

def reference(tokens, modulation, heights, w_in, w_x, w_dt, b_dt, a_log, d_skip, conv_w, conv_b, w_out, cotangent):
    params = (tokens.astype(jnp.float32), w_in.astype(jnp.float32), w_x.astype(jnp.float32), w_dt.astype(jnp.float32), b_dt, a_log, d_skip, conv_w, conv_b, w_out.astype(jnp.float32))

    def forward(x_all, win, wx, wdt, bdt, alog, dsk, cw, cb, wout):
        a_mat = -jnp.exp(alog)

        def per_item(pieces):
            x_item, mod_item, height = pieces
            return item_forward(x_item, mod_item, height, win, wx, wdt, bdt, a_mat, dsk, cw, cb, wout)
        return lax.map(jax.checkpoint(per_item), (x_all, modulation, heights))
    result, pull = jax.vjp(forward, *params)
    grads = pull(cotangent.astype(jnp.float32))
    return (result.astype(jnp.bfloat16), grads[0], grads[1], grads[2], grads[3], grads[4], grads[5], grads[6], grads[7], grads[8], grads[9])
```

```python
import jax
import jax.numpy as jnp
from jax import lax
from jax.experimental import pallas as pl
from jax.experimental.pallas import tpu as pltpu
from jax.sharding import PartitionSpec as P

epsilon = 1e-06
f32, bf16 = jnp.float32, jnp.bfloat16
LOG2E = 1.4426950408889634
CH = 16
N = 16
TB = 128

def dot(a, b): return lax.dot_general(a, b, (((1,), (0,)), ((), ())), preferred_element_type=f32)
def dot_t(a, b): return lax.dot_general(a, b, (((1,), (1,)), ((), ())), preferred_element_type=f32)

def scan_kernel(delta_ref, u_ref, bb_ref, cbd_ref, a2_ref, y_ref, s_ref, du_scr, st_scr):
    TB, C = delta_ref.shape
    L = C // 128
    i = pl.program_id(0)
    @pl.when(i == 0)
    def _():
        st_scr[...] = jnp.zeros_like(st_scr)
    du_scr[...] = delta_ref[...] * u_ref[...].astype(f32)
    s_ref[0, 0:N, :] = st_scr[...].astype(bf16)
    def chunk(k, st):
        base = pl.multiple_of(k * CH, CH)
        dref = delta_ref.at[pl.ds(base, CH), :]
        duref = du_scr.at[pl.ds(base, CH), :]
        bref = bb_ref.at[pl.ds(pl.multiple_of(base * N, CH * N), CH * N), :]
        sref = s_ref.at[0, pl.ds(pl.multiple_of(base * N + N, N), CH * N), :]
        st = list(st)
        for t in range(CH):
            b = bref[t * N:(t + 1) * N, :].astype(f32)
            for l in range(L):
                ls = slice(l * 128, (l + 1) * 128)
                d = jnp.broadcast_to(dref[t:t + 1, ls], (N, 128))
                w = jnp.broadcast_to(duref[t:t + 1, ls], (N, 128)) * b
                st[l] = jnp.exp2(d * a2_ref[:, ls]) * st[l] + w
                sref[t * N:(t + 1) * N, ls] = st[l].astype(bf16)
        y_ref[pl.ds(base, CH), :] = dot(cbd_ref[pl.ds(base, CH), :], sref[...])
        return tuple(st)
    st = tuple(st_scr[:, l * 128:(l + 1) * 128] for l in range(L))
    st = lax.fori_loop(0, TB // CH, chunk, st)
    for l in range(L):
        st_scr[:, l * 128:(l + 1) * 128] = st[l]

def scan_forward(delta, u, bb, cbd, a2):
    T, C = delta.shape
    nb = T // TB
    return pl.pallas_call(
        scan_kernel, grid=(nb,),
        in_specs=[pl.BlockSpec((TB, C), lambda i: (i, 0)), pl.BlockSpec((TB, C), lambda i: (i, 0)),
                  pl.BlockSpec((TB * N, 128), lambda i: (i, 0)), pl.BlockSpec((TB, CH * N), lambda i: (i, 0)),
                  pl.BlockSpec((N, C), lambda i: (0, 0))],
        out_specs=[pl.BlockSpec((TB, C), lambda i: (i, 0)), pl.BlockSpec((1, (TB + 1) * N, C), lambda i: (i, 0, 0))],
        out_shape=[jax.ShapeDtypeStruct((T, C), f32), jax.ShapeDtypeStruct((nb, (TB + 1) * N, C), bf16)],
        scratch_shapes=[pltpu.VMEM((TB, C), f32), pltpu.VMEM((N, C), f32)],
        compiler_params=pltpu.CompilerParams(vmem_limit_bytes=48 << 20),
        name="scan_out",
    )(delta, u, bb, cbd, a2)

def adjoint_kernel(delta_ref, u_ref, g_ref, cb_ref, bbd_ref, a2_ref, a_ref, sum_ref, s_ref,
               dd_ref, du_ref, db_ref, dc_ref, da_ref, dux, lam, ra, rd, dl_scr):
    TB, C = delta_ref.shape
    L = C // 128
    i = pl.program_id(0)
    @pl.when(i == 0)
    def _():
        dl_scr[...] = jnp.zeros_like(dl_scr)
        da_ref[...] = jnp.zeros_like(da_ref)
    dux[...] = (delta_ref[...] * u_ref[...].astype(f32)).astype(bf16)
    pick = (lax.broadcasted_iota(jnp.int32, (CH, CH * N), 1) // N == lax.broadcasted_iota(jnp.int32, (CH, CH * N), 0))
    def chunk(kk, dl):
        k = TB // CH - 1 - kk
        base = pl.multiple_of(k * CH, CH)
        rows = pl.ds(base, CH)
        dref = delta_ref.at[rows, :]
        gref = g_ref.at[rows, :]
        cref = cb_ref.at[pl.ds(pl.multiple_of(base * N, CH * N), CH * N), :]
        pref = s_ref.at[0, pl.ds(pl.multiple_of(base * N, N), CH * N), :]
        sref = s_ref.at[0, pl.ds(pl.multiple_of(base * N + N, N), CH * N), :]
        dl = list(dl)
        for t in reversed(range(CH)):
            rs = slice(t * N, (t + 1) * N)
            c = cref[rs, :].astype(f32)
            for l in range(L):
                ls = slice(l * 128, (l + 1) * 128)
                d = jnp.broadcast_to(dref[t:t + 1, ls], (N, 128))
                g = jnp.broadcast_to(gref[t:t + 1, ls], (N, 128)).astype(f32)
                lm = dl[l] + g * c
                dl[l] = jnp.exp2(d * a2_ref[:, ls]) * lm
                lam[rs, ls] = lm.astype(bf16)
                r = dl[l].astype(bf16) * pref[rs, ls]
                ra[rs, ls] = r * a_ref[:, ls]
                rd[rs, ls] = r * d.astype(bf16)
        ddu = dot(bbd_ref[rows, :], lam[...])
        dda = dot(sum_ref[0:CH, :], ra[...])
        da_ref[...] += dot(sum_ref[CH:2 * CH, :], rd[...])
        dbm = dot_t(dux[rows, :], lam[...])
        dcm = dot_t(gref[...].astype(bf16), sref[...])
        db_ref[k] = jnp.sum(jnp.where(pick, dbm, 0.0), axis=0, keepdims=True)
        dc_ref[k] = jnp.sum(jnp.where(pick, dcm, 0.0), axis=0, keepdims=True)
        dd_ref[rows, :] = dda + u_ref[rows, :].astype(f32) * ddu
        du_ref[rows, :] = (dref[...] * ddu).astype(du_ref.dtype)
        return tuple(dl)
    dl = tuple(dl_scr[:, l * 128:(l + 1) * 128] for l in range(L))
    dl = lax.fori_loop(0, TB // CH, chunk, dl)
    for l in range(L):
        dl_scr[:, l * 128:(l + 1) * 128] = dl[l]

def scan_adjoint(delta, u, g, cb, bbd, a2, a16, S, du_dtype=f32):
    T, C = delta.shape
    nb = T // TB
    q = jnp.arange(CH * N)
    sums = jnp.concatenate([(q[None, :] // N == jnp.arange(CH)[:, None]), (q[None, :] % N == jnp.arange(N)[:, None])]).astype(bf16)
    rev = lambda i: (nb - 1 - i, 0)
    rev3 = lambda i: (nb - 1 - i, 0, 0)
    zero = lambda i: (0, 0)
    return pl.pallas_call(
        adjoint_kernel, grid=(nb,),
        in_specs=[pl.BlockSpec((TB, C), rev), pl.BlockSpec((TB, C), rev), pl.BlockSpec((TB, C), rev),
                  pl.BlockSpec((TB * N, 128), rev), pl.BlockSpec((TB, CH * N), rev),
                  pl.BlockSpec((N, C), zero), pl.BlockSpec((N, C), zero), pl.BlockSpec((2 * CH, CH * N), zero),
                  pl.BlockSpec((1, (TB + 1) * N, C), rev3)],
        out_specs=[pl.BlockSpec((TB, C), rev), pl.BlockSpec((TB, C), rev),
                   pl.BlockSpec((TB // CH, 1, CH * N), rev3), pl.BlockSpec((TB // CH, 1, CH * N), rev3),
                   pl.BlockSpec((N, C), zero)],
        out_shape=[jax.ShapeDtypeStruct((T, C), f32), jax.ShapeDtypeStruct((T, C), du_dtype),
                   jax.ShapeDtypeStruct((T // CH, 1, CH * N), f32), jax.ShapeDtypeStruct((T // CH, 1, CH * N), f32),
                   jax.ShapeDtypeStruct((N, C), f32)],
        scratch_shapes=[pltpu.VMEM((TB, C), bf16), pltpu.VMEM((CH * N, C), bf16), pltpu.VMEM((CH * N, C), bf16),
                        pltpu.VMEM((CH * N, C), bf16), pltpu.VMEM((N, C), f32)],
        compiler_params=pltpu.CompilerParams(vmem_limit_bytes=48 << 20),
        name="scan_back",
    )(delta, u, g, cb, bbd, a2, a16, sums, S)

def blockdiag(m):
    T = m.shape[0]
    tl = jnp.tile(m, (1, CH))
    keep = (jnp.arange(CH * N)[None, :] // N) == (jnp.arange(T)[:, None] % CH)
    return jnp.where(keep, tl, 0).astype(bf16)
def lanes(m):
    T = m.shape[0]
    return jnp.broadcast_to(m.reshape(T * N, 1), (T * N, 128)).astype(bf16)


def silu_slope(value):
    sigmoid = jax.nn.sigmoid(value)
    return sigmoid * (1.0 + value * (1.0 - sigmoid))


def normalize(rows_in, shift, scale):
    mean = jnp.mean(rows_in, axis=-1, keepdims=True)
    centered = rows_in - mean
    variance = jnp.mean(centered * centered, axis=-1, keepdims=True)
    return centered * lax.rsqrt(variance + epsilon) * (1.0 + scale) + shift


def partner(block, axis, bit):
    return lax.ppermute(block, axis, [(i, i ^ bit) for i in range(lax.axis_size(axis))])


def bits_down(axis):
    bit = lax.axis_size(axis) // 2
    while bit:
        yield bit
        bit //= 2


def bits_up(axis):
    return reversed(list(bits_down(axis)))


def gather_rows(block, axis, bits):
    index = lax.axis_index(axis)
    size = lax.axis_size(axis)
    held = block[(None,) * len(bits)]
    places = [b.bit_length() - 1 for b in bits]
    for bit, place in zip(bits, places):
        other = partner(held, axis, bit)
        dim = len(bits) - 1 - place
        upper = (index & bit) != 0
        held = jnp.concatenate([jnp.where(upper, other, held), jnp.where(upper, held, other)], axis=dim)
    return held.reshape((size,) + block.shape)


def scatter_sum(blocks, axis, bits):
    index = lax.axis_index(axis)
    count = len(bits)
    held = blocks.reshape((2,) * count + blocks.shape[1:])
    for bit in bits:
        dim = count - 1 - (bit.bit_length() - 1)
        mine = (index & bit) // bit
        keep = lax.dynamic_index_in_dim(held, mine, dim, keepdims=True)
        send = lax.dynamic_index_in_dim(held, 1 - mine, dim, keepdims=True).astype(bf16)
        held = keep.astype(f32) + partner(send, axis, bit).astype(f32)
    return held.reshape(blocks.shape[1:])


def sum_seq(value):
    index = lax.axis_index("seq")
    rows = value.shape[0] // 2
    halves = value.reshape((2, rows) + value.shape[1:])
    mine = index & 1
    held = lax.dynamic_index_in_dim(halves, mine, 0, keepdims=False) + partner(
        lax.dynamic_index_in_dim(halves, 1 - mine, 0, keepdims=False), "seq", 1
    )
    bit = 2
    while bit < lax.axis_size("seq"):
        held = held + partner(held, "seq", bit)
        bit *= 2
    other = partner(held, "seq", 1)
    upper = mine != 0
    return jnp.concatenate([jnp.where(upper, other, held), jnp.where(upper, held, other)], axis=0)


def across_seq(blocks):
    return lax.all_to_all(blocks, "seq", split_axis=0, concat_axis=0, tiled=True)


def contract_rows(left, right):
    return lax.dot_general(left, right, (((0,), (0,)), ((), ())), preferred_element_type=f32)


def diagonal_rows(value):
    return value.reshape(-1, N)


def shards(
    tokens,
    modulation,
    heights,
    w_in,
    w_x,
    w_dt,
    b_dt,
    a_log,
    d_skip,
    conv_w,
    conv_b,
    w_out,
    cotangent,
):
    _, seq_len, width = tokens.shape
    parts = lax.axis_size("seq")
    data_parts = lax.axis_size("dp")
    inner = w_out.shape[0]
    chans = inner // parts
    rank = w_dt.shape[1]
    taps = conv_w.shape[1]
    total = seq_len * parts
    part = lax.axis_index("seq")
    seq_down, seq_up = list(bits_down("seq")), list(bits_up("seq"))
    dp_down, dp_up = list(bits_down("dp")), list(bits_up("dp"))

    def own(array, axis=0, offset=0):
        return lax.dynamic_slice_in_dim(array, offset + part * chans, chans, axis)

    w_conv_in, w_gate_in = own(w_in, 1), own(w_in, 1, inner)
    wx, wdt, bdt, wout = own(w_x), own(w_dt), own(b_dt), own(w_out)
    dsk, cw, cb = own(d_skip), own(conv_w), own(conv_b)
    a_state = -jnp.exp(own(a_log).T)
    a_two = a_state * LOG2E
    a_low = a_state.astype(bf16)
    shift, scale, gate = modulation[0, 0:1], modulation[0, 1:2], modulation[0, 2:3]

    x_own = tokens[0].astype(f32)
    normed, norm_back = jax.vjp(lambda rows_in: normalize(rows_in, shift, scale), x_own)
    hmod = gather_rows(normed.astype(bf16), "seq", seq_down).reshape(total, width)
    d_res = cotangent[0].astype(f32)
    d_branch = gather_rows((gate * d_res).astype(bf16), "seq", seq_down).reshape(total, width)

    x_conv = dot(hmod, w_conv_in).astype(bf16)
    z_gate = dot(hmod, w_gate_in)
    padded = jnp.concatenate([jnp.zeros((taps - 1, chans), bf16), x_conv], axis=0).astype(f32)
    pre_conv = cb + sum(padded[k : k + total] * cw[:, k] for k in range(taps))
    u_low = jax.nn.silu(pre_conv).astype(bf16)
    proj = sum_seq(dot(u_low, wx)).astype(bf16)

    height = heights[0]
    wide = total // height
    column = total - 1 - jnp.arange(total, dtype=jnp.int32)
    order = column % height * wide + column // height
    to_columns = (order[:, None] == jnp.arange(total, dtype=jnp.int32)[None, :]).astype(bf16)

    def columns_of(value):
        return dot(to_columns, value).astype(bf16)

    def rows_of(value):
        return contract_rows(to_columns, value)

    u_col = columns_of(u_low)
    proj_col = columns_of(proj)

    def terms(p):
        pre = dot_t(p[:, :rank], wdt) + bdt
        b_mat, c_mat = p[:, rank : rank + N], p[:, rank + N :]
        return (jax.nn.softplus(pre), lanes(b_mat), lanes(c_mat), blockdiag(b_mat), blockdiag(c_mat))

    delta_row, bl_row, cl_row, bd_row, cd_row = terms(proj)
    delta_col, bl_col, cl_col, bd_col, cd_col = terms(proj_col)
    y_fwd, s_row = scan_forward(delta_row, u_low, bl_row, cd_row, a_two)
    y_col, s_col = scan_forward(delta_col, u_col, bl_col, cd_col, a_two)
    u_full = u_low.astype(f32)
    y_all = y_fwd + rows_of(y_col.astype(bf16)) + dsk * u_full
    silu_z = jax.nn.silu(z_gate)
    gated = (y_all * silu_z).astype(bf16)
    branch = scatter_sum(dot(gated, wout).astype(bf16).reshape(parts, seq_len, width), "seq", seq_up)
    result = (x_own + gate * branch).astype(bf16)

    d_gated = dot_t(d_branch, wout)
    d_y = d_gated * silu_z
    d_z = (d_gated * y_all * silu_slope(z_gate)).astype(bf16)
    g_dskip = jnp.sum(d_y * u_full, axis=0)
    g_out = contract_rows(gated, d_branch).astype(bf16)
    g_gate = contract_rows(hmod, d_z).astype(bf16)

    def by_owner(grad):
        shaped = grad.reshape(parts, data_parts, width // (parts * data_parts), chans)
        return shaped.swapaxes(0, 1)

    out_sum = lax.psum_scatter(g_out, "dp", scatter_dimension=0, tiled=True)
    g_out = lax.all_gather(out_sum.astype(bf16), "dp", axis=0, tiled=True).astype(f32)
    gate_sum = lax.psum_scatter(by_owner(g_gate), "dp", scatter_dimension=0, tiled=True)[0]
    gate_sum = across_seq(gate_sum.astype(bf16)).swapaxes(0, 1)
    g_gate = lax.all_gather(gate_sum, "dp", axis=0, tiled=True).reshape(width // parts, inner).astype(f32)

    dy_col = columns_of(d_y.astype(bf16))
    dd_col, du_col, db_col, dc_col, da_col = scan_adjoint(
        delta_col, u_col, dy_col, cl_col, bd_col, a_two, a_low, s_col, bf16
    )
    dd_row, du_row, db_row, dc_row, da_row = scan_adjoint(
        delta_row, u_low, d_y, cl_row, bd_row, a_two, a_low, s_row, f32
    )

    def low_grads(dd, delta, p, db, dc):
        d_pre = dd * -jnp.expm1(-delta)
        low_pre = d_pre.astype(bf16)
        grad = jnp.concatenate([dot(low_pre, wdt), diagonal_rows(db), diagonal_rows(dc)], axis=1)
        return grad, contract_rows(low_pre, p[:, :rank]), jnp.sum(d_pre, axis=0)

    p_col, gw_col, gb_col = low_grads(dd_col, delta_col, proj_col, db_col, dc_col)
    p_row, gw_row, gb_row = low_grads(dd_row, delta_row, proj, db_row, dc_row)
    d_projs = sum_seq(jnp.concatenate([p_row, p_col], axis=1))
    d_proj = (d_projs[:, : p_row.shape[1]] + rows_of(d_projs[:, p_row.shape[1] :].astype(bf16))).astype(bf16)
    g_wx = contract_rows(u_low, d_proj)
    d_u = du_row + rows_of(du_col) + d_y * dsk + dot_t(d_proj, wx)
    d_pre_conv = d_u * silu_slope(pre_conv)
    g_convb = jnp.sum(d_pre_conv, axis=0)
    g_convw = jnp.stack(
        [jnp.sum(padded[k : k + total] * d_pre_conv, axis=0) for k in range(taps)], axis=1
    )
    later = jnp.concatenate([d_pre_conv, jnp.zeros((taps - 1, chans), f32)], axis=0)
    d_xconv = sum(cw[:, k] * later[taps - 1 - k : taps - 1 - k + total] for k in range(taps)).astype(bf16)

    g_conv_in = by_owner(contract_rows(hmod, d_xconv).astype(bf16))
    rows_each = parts * g_conv_in.shape[2]
    small = jnp.concatenate(
        [
            g_wx,
            gw_row + gw_col,
            ((da_row + da_col) * a_state).T,
            (gb_row + gb_col)[:, None],
            g_dskip[:, None],
            g_convb[:, None],
            g_convw,
        ],
        axis=1,
    )
    columns = small.shape[1]
    small = jnp.pad(small, ((0, 0), (0, -columns % 128))).astype(bf16)
    small = small.reshape(data_parts, -1, chans)
    payload = jnp.concatenate([g_conv_in.reshape(data_parts, rows_each, chans), small], axis=1)
    held = scatter_sum(payload, "dp", dp_up).astype(bf16)
    mine = across_seq(held[:rows_each].reshape(parts, -1, chans)).swapaxes(0, 1)
    held = jnp.concatenate([mine.reshape(rows_each, chans), held[rows_each:]], axis=0)
    held = gather_rows(held, "dp", dp_down)
    g_conv_in = held[:, :rows_each].reshape(width // parts, inner).astype(f32)
    small = held[:, rows_each:].reshape(chans, -1).astype(f32)

    d_h = dot_t(d_xconv, w_conv_in) + dot_t(d_z, w_gate_in)
    d_h = scatter_sum(d_h.astype(bf16).reshape(parts, seq_len, width), "seq", seq_up)
    d_x = d_res + norm_back(d_h)[0]

    edges = [0]
    for size in (w_x.shape[1], rank, N, 1, 1, 1, taps):
        edges.append(edges[-1] + size)
    pieces = [small[:, lo:hi] for lo, hi in zip(edges, edges[1:])]
    return (
        result[None],
        d_x[None],
        jnp.concatenate([g_conv_in, g_gate], axis=1),
        pieces[0],
        pieces[1],
        pieces[3][:, 0],
        pieces[2],
        pieces[4][:, 0],
        pieces[6],
        pieces[5][:, 0],
        g_out,
    )


def solution(mesh):
    placed = (
        P("dp", "seq", None),
        P("dp", None, None),
        P("dp"),
        P(),
        P(),
        P(),
        P(),
        P(),
        P(),
        P(),
        P(),
        P(),
        P("dp", "seq", None),
    )
    return jax.shard_map(
        shards,
        mesh=mesh,
        in_specs=placed,
        out_specs=(
            P("dp", "seq", None),
            P("dp", "seq", None),
            P("seq", None),
            P("seq", None),
            P("seq", None),
            P("seq"),
            P("seq", None),
            P("seq"),
            P("seq", None),
            P("seq"),
            P("seq", None),
        ),
        check_vma=False,
    )
```

```python
import jax
import jax.numpy as jnp
from jax import lax
from jax.experimental import pallas as pl
from jax.experimental.pallas import tpu as pltpu
from jax.sharding import PartitionSpec as P

epsilon = 1e-06
f32, bf16 = jnp.float32, jnp.bfloat16
LOG2E = 1.4426950408889634
N = 16
CH = 16
TB = 128
GROUP = 4


def dot(a, b):
    return lax.dot_general(a, b, (((1,), (0,)), ((), ())), preferred_element_type=f32)


def dot_t(a, b):
    return lax.dot_general(a, b, (((1,), (1,)), ((), ())), preferred_element_type=f32)


def contract_rows(left, right):
    return lax.dot_general(left, right, (((0,), (0,)), ((), ())), preferred_element_type=f32)


def tiles(width):
    return [slice(lo, lo + 128) for lo in range(0, width, 128)]


def across(row):
    return jnp.broadcast_to(row, (N, row.shape[1]))


def along(column):
    return jnp.broadcast_to(column, (N, 128))


def tree(values):
    while len(values) > 1:
        values = [a + b for a, b in zip(values[::2], values[1::2])] + values[len(values) & ~1 :]
    return values[0]


def places(shape, dim):
    return lax.broadcasted_iota(jnp.int32, shape, dim)


def spread(p, first):
    shape = (p.shape[1], CH * N)
    choose = (places(shape, 0) == first + places(shape, 1) % N).astype(bf16)
    shape = (p.shape[0], CH * N)
    keep = places(shape, 1) // N == places(shape, 0) % CH
    return jnp.where(keep, dot(p, choose), 0.0).astype(bf16)


def turned(p, first):
    shape = (N, p.shape[1])
    choose = (places(shape, 1) == first + places(shape, 0)).astype(bf16)
    return dot_t(choose, p)


def group_columns(mat, group):
    return pltpu.roll(mat, (TB - group * GROUP * CH) % TB, 1)


def work(steps):
    return pl.CostEstimate(flops=100 * steps, bytes_accessed=steps // 4, transcendentals=0)


def scan_kernel(p_ref, u_ref, wdt_ref, bdt_ref, a_ref, y_ref, s_ref, delta_ref, du_scr, cd_scr, state_scr):
    lanes = tiles(delta_ref.shape[1])
    rank = p_ref.shape[1] - 2 * N

    @pl.when(pl.program_id(0) == 0)
    def _():
        state_scr[...] = jnp.zeros_like(state_scr)

    p = p_ref[...]
    pre = dot_t(p, wdt_ref[...]) + bdt_ref[...]
    delta = jnp.maximum(pre, 0.0) + jnp.log1p(jnp.exp(-jnp.abs(pre)))
    delta_ref[...] = delta
    du_scr[...] = delta * u_ref[...].astype(f32)
    cd_scr[...] = spread(p, rank + N)
    b_turned = turned(p, rank)
    s_ref[0, 0:N, :] = state_scr[...].astype(bf16)

    def group(step, state):
        b_all = group_columns(b_turned, step)
        state = list(state)
        for j in range(GROUP):
            base = pl.multiple_of((step * GROUP + j) * CH, CH)
            rows = pl.ds(base, CH)
            d_view = delta_ref.at[rows, :]
            du_view = du_scr.at[rows, :]
            s_view = s_ref.at[0, pl.ds(pl.multiple_of(base * N + N, N), CH * N), :]
            for t in range(CH):
                b = along(b_all[:, j * CH + t : j * CH + t + 1])
                for i, ls in enumerate(lanes):
                    decay = jnp.exp2(across(d_view[t : t + 1, ls]) * a_ref[:, ls])
                    state[i] = decay * state[i] + across(du_view[t : t + 1, ls]) * b
                    s_view[t * N : (t + 1) * N, ls] = state[i].astype(bf16)
            y_ref[rows, :] = dot(cd_scr[rows, :], s_view[...]).astype(y_ref.dtype)
        return tuple(state)

    state = lax.fori_loop(0, TB // CH // GROUP, group, tuple(state_scr[:, ls] for ls in lanes))
    for i, ls in enumerate(lanes):
        state_scr[:, ls] = state[i]


def scan_forward(p, u, wdt, bdt, a_two, y_dtype):
    total, chans = u.shape
    blocks = total // TB
    rows = lambda i: (i, 0)
    whole = lambda i: (0, 0)
    wide = pl.BlockSpec((TB, chans), rows)
    return pl.pallas_call(
        scan_kernel,
        grid=(blocks,),
        in_specs=[
            pl.BlockSpec((TB, p.shape[1]), rows),
            wide,
            pl.BlockSpec(wdt.shape, whole),
            pl.BlockSpec((1, chans), whole),
            pl.BlockSpec((N, chans), whole),
        ],
        out_specs=[wide, pl.BlockSpec((1, (TB + 1) * N, chans), lambda i: (i, 0, 0)), wide],
        out_shape=[
            jax.ShapeDtypeStruct((total, chans), y_dtype),
            jax.ShapeDtypeStruct((blocks, (TB + 1) * N, chans), bf16),
            jax.ShapeDtypeStruct((total, chans), f32),
        ],
        scratch_shapes=[
            pltpu.VMEM((TB, chans), f32),
            pltpu.VMEM((TB, CH * N), bf16),
            pltpu.VMEM((N, chans), f32),
        ],
        compiler_params=pltpu.CompilerParams(vmem_limit_bytes=40 << 20),
        cost_estimate=work(20 * total * chans * N),
        name="scan_out",
    )(p, u, wdt, bdt, a_two)


def lane_sums(part):
    sums = dot_t(jnp.ones((16, 128), bf16), part)[0:8]
    own = places((8, 128), 1) // N == places((8, 128), 0)
    rows = []
    for lo in range(0, part.shape[0], 128):
        held = jnp.where(own, sums[:, lo : lo + 128], 0.0)
        for shift in (64, 32, 16):
            held = held + pltpu.roll(held, shift, 1)
        rows.append(held)
    return jnp.concatenate(rows, axis=0)


def adjoint_kernel(
    p_ref, delta_ref, u_ref, g_ref, wdt_ref, a_ref, alow_ref, s_ref,
    du_ref, dp_ref, gw_ref, gb_ref, da_ref,
    dux, bd_scr, dd_scr, lam, ra, pb, pc, carry,
):
    lanes = tiles(delta_ref.shape[1])
    rank = p_ref.shape[1] - 2 * N

    @pl.when(pl.program_id(0) == 0)
    def _():
        for ref in (carry, da_ref, gw_ref, gb_ref):
            ref[...] = jnp.zeros_like(ref)

    p = p_ref[...]
    dux[...] = delta_ref[...] * u_ref[...].astype(f32)
    bd_scr[...] = spread(p, rank)
    c_turned = turned(p, rank + N)
    adder = (places((CH, CH * N), 1) // N == places((CH, CH * N), 0)).astype(bf16)

    def back(base, j, c_cols, held):
        d_view = delta_ref.at[pl.ds(base, CH), :]
        g_view = g_ref.at[pl.ds(base, CH), :]
        du_view = dux.at[pl.ds(base, CH), :]
        before = s_ref.at[0, pl.ds(pl.multiple_of(base * N, N), (CH + 1) * N), :]
        states = pl.ds(pl.multiple_of(base * N, CH * N), CH * N)
        pb_view, pc_view = pb.at[states, :], pc.at[states, :]
        held, pair, total = list(held), [None] * len(lanes), [None] * len(lanes)
        for t in reversed(range(CH)):
            rs = slice(t * N, (t + 1) * N)
            after = slice((t + 1) * N, (t + 2) * N)
            c = along(c_cols[:, t : t + 1])
            sum_b, sum_c = [], []
            for i, ls in enumerate(lanes):
                d = across(d_view[t : t + 1, ls])
                g = across(g_view[t : t + 1, ls]).astype(f32)
                grad = held[i] + g * c
                held[i] = jnp.exp2(d * a_ref[:, ls]) * grad
                lam[j, rs, ls] = grad.astype(bf16)
                r = held[i].astype(bf16) * before[rs, ls]
                ra[j, rs, ls] = r * alow_ref[:, ls]
                rd = r * d.astype(bf16)
                if t % 2:
                    pair[i] = rd
                else:
                    both = (pair[i] + rd).astype(f32)
                    total[i] = both if total[i] is None else total[i] + both
                sum_b.append(grad * across(du_view[t : t + 1, ls]))
                sum_c.append(before[after, ls] * g.astype(bf16))
            pb_view[rs, :] = tree(sum_b).astype(bf16)
            pc_view[rs, :] = tree(sum_c).astype(bf16)
        for i, ls in enumerate(lanes):
            da_ref[:, ls] += total[i]
        return tuple(held)

    def sums(base, j):
        rows = pl.ds(base, CH)
        d_in = dot(bd_scr[rows, :], lam[j])
        d_exp = dot(adder, ra[j])
        dd_scr[rows, :] = d_exp + u_ref[rows, :].astype(f32) * d_in
        du_ref[rows, :] = (delta_ref[rows, :] * d_in).astype(du_ref.dtype)

    def group(step, held):
        place = TB // CH // GROUP - 1 - step
        c_all = group_columns(c_turned, place)
        for j in reversed(range(GROUP)):
            base = pl.multiple_of((place * GROUP + j) * CH, CH)
            held = back(base, j, c_all[:, j * CH : (j + 1) * CH], held)
            sums(base, j)
        return held

    held = lax.fori_loop(0, TB // CH // GROUP, group, tuple(carry[:, ls] for ls in lanes))
    for i, ls in enumerate(lanes):
        carry[:, ls] = held[i]
    delta = delta_ref[...]
    slope = jnp.where(
        delta < 0.01, delta * (1.0 - delta * (0.5 - delta * (1.0 / 6.0))), 1.0 - jnp.exp(-delta)
    )
    d_pre = dd_scr[...] * slope
    gb_ref[...] += jnp.sum(d_pre, axis=0, keepdims=True)
    d_pre = d_pre.astype(bf16)
    gw_ref[...] += contract_rows(d_pre, p)
    d_low = dot(d_pre, wdt_ref[...])
    lane = places(d_low.shape, 1)
    tail = jnp.where(lane < rank + N, lane_sums(pb[...]), lane_sums(pc[...]))
    dp_ref[...] = jnp.where(lane < rank, d_low, tail)


def scan_adjoint(p, delta, u, g, wdt, a_two, a_low, states, du_dtype):
    total, chans = delta.shape
    blocks = total // TB
    rows = lambda i: (blocks - 1 - i, 0)
    first = lambda i: (blocks - 1 - i, 0, 0)
    whole = lambda i: (0, 0)
    wide = pl.BlockSpec((TB, chans), rows)
    narrow = pl.BlockSpec((TB, p.shape[1]), rows)
    per_state = pl.BlockSpec((N, chans), whole)
    return pl.pallas_call(
        adjoint_kernel,
        grid=(blocks,),
        in_specs=[
            narrow,
            wide,
            wide,
            wide,
            pl.BlockSpec(wdt.shape, whole),
            per_state,
            per_state,
            pl.BlockSpec((1, (TB + 1) * N, chans), first),
        ],
        out_specs=[
            wide,
            narrow,
            pl.BlockSpec(wdt.shape, whole),
            pl.BlockSpec((1, chans), whole),
            per_state,
        ],
        out_shape=[
            jax.ShapeDtypeStruct((total, chans), du_dtype),
            jax.ShapeDtypeStruct(p.shape, f32),
            jax.ShapeDtypeStruct(wdt.shape, f32),
            jax.ShapeDtypeStruct((1, chans), f32),
            jax.ShapeDtypeStruct((N, chans), f32),
        ],
        scratch_shapes=[
            pltpu.VMEM((TB, chans), f32),
            pltpu.VMEM((TB, CH * N), bf16),
            pltpu.VMEM((TB, chans), f32),
            pltpu.VMEM((GROUP, CH * N, chans), bf16),
            pltpu.VMEM((GROUP, CH * N, chans), bf16),
            pltpu.VMEM((TB * N, 128), bf16),
            pltpu.VMEM((TB * N, 128), bf16),
            pltpu.VMEM((N, chans), f32),
        ],
        compiler_params=pltpu.CompilerParams(vmem_limit_bytes=48 << 20),
        cost_estimate=work(40 * total * chans * N),
        name="scan_back",
    )(p, delta, u, g, wdt, a_two, a_low, states)


def silu_slope(value):
    sigmoid = jax.nn.sigmoid(value)
    return sigmoid * (1.0 + value * (1.0 - sigmoid))


def normalize(rows_in, shift, scale):
    mean = jnp.mean(rows_in, axis=-1, keepdims=True)
    centered = rows_in - mean
    variance = jnp.mean(centered * centered, axis=-1, keepdims=True)
    return centered * lax.rsqrt(variance + epsilon) * (1.0 + scale) + shift


def partner(block, axis, bit):
    return lax.ppermute(block, axis, [(i, i ^ bit) for i in range(lax.axis_size(axis))])


def bits_down(axis):
    bit = lax.axis_size(axis) // 2
    while bit:
        yield bit
        bit //= 2


def bits_up(axis):
    return reversed(list(bits_down(axis)))


def gather_rows(block, axis, bits):
    index = lax.axis_index(axis)
    size = lax.axis_size(axis)
    held = block[(None,) * len(bits)]
    places = [b.bit_length() - 1 for b in bits]
    for bit, place in zip(bits, places):
        other = partner(held, axis, bit)
        dim = len(bits) - 1 - place
        upper = (index & bit) != 0
        held = jnp.concatenate([jnp.where(upper, other, held), jnp.where(upper, held, other)], axis=dim)
    return held.reshape((size,) + block.shape)


def split_bits(blocks, bits):
    return blocks.reshape((2,) * len(bits) + blocks.shape[1:])


def scatter_hop(held, axis, bits, hop):
    bit = bits[hop]
    dim = len(bits) - 1 - (bit.bit_length() - 1)
    mine = (lax.axis_index(axis) & bit) // bit
    keep = lax.dynamic_index_in_dim(held, mine, dim, keepdims=True)
    send = lax.dynamic_index_in_dim(held, 1 - mine, dim, keepdims=True).astype(bf16)
    return keep.astype(f32) + partner(send, axis, bit).astype(f32)


def scatter_sum(blocks, axis, bits):
    held = split_bits(blocks, bits)
    for hop in range(len(bits)):
        held = scatter_hop(held, axis, bits, hop)
    return held.reshape(blocks.shape[1:])


def sum_seq(value):
    index = lax.axis_index("seq")
    rows = value.shape[0] // 2
    halves = value.reshape((2, rows) + value.shape[1:])
    mine = index & 1
    held = lax.dynamic_index_in_dim(halves, mine, 0, keepdims=False) + partner(
        lax.dynamic_index_in_dim(halves, 1 - mine, 0, keepdims=False), "seq", 1
    )
    bit = 2
    while bit < lax.axis_size("seq"):
        held = held + partner(held, "seq", bit)
        bit *= 2
    other = partner(held, "seq", 1)
    upper = mine != 0
    return jnp.concatenate([jnp.where(upper, other, held), jnp.where(upper, held, other)], axis=0)


def sum_pair(first, second):
    odd = (lax.axis_index("seq") & 1) != 0
    held = jnp.where(odd, second, first) + partner(jnp.where(odd, first, second), "seq", 1)
    bit = 2
    while bit < lax.axis_size("seq"):
        held = held + partner(held, "seq", bit)
        bit *= 2
    other = partner(held, "seq", 1)
    return jnp.where(odd, other, held), jnp.where(odd, held, other)


def across_seq(blocks):
    return lax.all_to_all(blocks, "seq", split_axis=0, concat_axis=0, tiled=True)


def join_out(early, rows_each, chans):
    owners, _, strip = early.shape
    sides = rows_each * owners // chans
    rows = chans // owners

    def kernel(in_ref, out_ref):
        for k in range(sides):
            out_ref[:, k * strip : (k + 1) * strip] = in_ref[0, k * rows : (k + 1) * rows, :].astype(f32)

    if rows % 16:
        blocks = early[:, :rows_each].reshape(owners, sides, rows, strip).swapaxes(1, 2)
        return blocks.reshape(chans, sides * strip).astype(f32)
    return pl.pallas_call(
        kernel,
        grid=(owners,),
        in_specs=[pl.BlockSpec((1, rows_each, strip), lambda i: (i, 0, 0))],
        out_specs=pl.BlockSpec((rows, sides * strip), lambda i: (i, 0)),
        out_shape=jax.ShapeDtypeStruct((chans, sides * strip), f32),
        cost_estimate=pl.CostEstimate(flops=0, bytes_accessed=24 << 20, transcendentals=0),
        name="join_out",
    )(early)


def join_gate(early, rows_each, inner, parts):
    owners, _, chans = early.shape
    rows = rows_each // parts

    def kernel(in_ref, out_ref):
        for k in range(parts):
            out_ref[:, k * chans : (k + 1) * chans] = in_ref[0, k * rows : (k + 1) * rows, :].astype(f32)

    if rows % 16:
        blocks = early[:, rows_each:].reshape(owners, parts, rows, chans).swapaxes(1, 2)
        return blocks.reshape(owners * rows, inner).astype(f32)
    return pl.pallas_call(
        kernel,
        grid=(owners,),
        in_specs=[pl.BlockSpec((1, rows_each, chans), lambda i: (i, 1, 0))],
        out_specs=pl.BlockSpec((rows, inner), lambda i: (i, 1)),
        out_shape=jax.ShapeDtypeStruct((owners * rows, 2 * inner), f32),
        cost_estimate=pl.CostEstimate(flops=0, bytes_accessed=24 << 20, transcendentals=0),
        name="join_gate",
    )(early)


def join_in(gate_half, left, right, parts):
    owners, rows_each, half = left.shape
    rows = rows_each // parts

    def kernel(left_ref, right_ref, _, out_ref):
        for k in range(parts):
            for side, ref in enumerate((left_ref, right_ref)):
                lo = (2 * k + side) * half
                out_ref[:, lo : lo + half] = ref[0, k * rows : (k + 1) * rows, :].astype(f32)

    if rows % 16:
        both = jnp.concatenate([left, right[:, :rows_each]], axis=2)
        both = both.reshape(owners, parts, rows, 2 * half).swapaxes(1, 2).reshape(owners * rows, -1)
        return jnp.concatenate([both.astype(f32), gate_half], axis=1)
    block = pl.BlockSpec((1, rows_each, half), lambda i: (i, 0, 0))
    return pl.pallas_call(
        kernel,
        grid=(owners,),
        in_specs=[block, block, pl.BlockSpec(memory_space=pl.ANY)],
        out_specs=pl.BlockSpec((rows, 2 * half * parts), lambda i: (i, 0)),
        out_shape=jax.ShapeDtypeStruct(gate_half.shape, f32),
        input_output_aliases={2: 0},
        cost_estimate=pl.CostEstimate(flops=0, bytes_accessed=24 << 20, transcendentals=0),
        name="join_in",
    )(left, right, gate_half)


def shards(
    tokens,
    modulation,
    heights,
    w_in,
    w_x,
    w_dt,
    b_dt,
    a_log,
    d_skip,
    conv_w,
    conv_b,
    w_out,
    cotangent,
):
    _, seq_len, width = tokens.shape
    parts = lax.axis_size("seq")
    data_parts = lax.axis_size("dp")
    inner = w_out.shape[0]
    chans = inner // parts
    rank = w_dt.shape[1]
    taps = conv_w.shape[1]
    total = seq_len * parts
    part = lax.axis_index("seq")
    seq_down, seq_up = list(bits_down("seq")), list(bits_up("seq"))
    dp_down, dp_up = list(bits_down("dp")), list(bits_up("dp"))

    def own(array, axis=0, offset=0):
        return lax.dynamic_slice_in_dim(array, offset + part * chans, chans, axis)

    w_conv_in, w_gate_in = own(w_in, 1), own(w_in, 1, inner)
    wx, wdt, bdt, wout = own(w_x), own(w_dt), own(b_dt)[None], own(w_out)
    wdt = jnp.pad(wdt, ((0, 0), (0, 2 * N)))
    dsk, cw, cb = own(d_skip), own(conv_w), own(conv_b)
    a_state = -jnp.exp(own(a_log).T)
    a_two = a_state * LOG2E
    a_low = a_state.astype(bf16)
    shift, scale, gate = modulation[0, 0:1], modulation[0, 1:2], modulation[0, 2:3]

    x_own = tokens[0].astype(f32)
    normed, norm_back = jax.vjp(lambda rows_in: normalize(rows_in, shift, scale), x_own)
    hmod = gather_rows(normed.astype(bf16), "seq", seq_down).reshape(total, width)
    d_res = cotangent[0].astype(f32)

    x_conv = dot(hmod, w_conv_in).astype(bf16)
    z_gate = dot(hmod, w_gate_in)
    padded = jnp.concatenate([jnp.zeros((taps - 1, chans), bf16), x_conv], axis=0).astype(f32)
    pre_conv = cb + sum(padded[k : k + total] * cw[:, k] for k in range(taps))
    u_low = jax.nn.silu(pre_conv).astype(bf16)
    proj = sum_seq(dot(u_low, wx)).astype(bf16)

    height = heights[0]
    wide = total // height
    column = total - 1 - jnp.arange(total, dtype=jnp.int32)
    order = column % height * wide + column // height
    to_columns = (order[:, None] == jnp.arange(total, dtype=jnp.int32)[None, :]).astype(bf16)

    def columns_of(value):
        return dot(to_columns, value).astype(bf16)

    def rows_of(value):
        return contract_rows(to_columns, value)

    u_col = columns_of(u_low)
    proj_col = columns_of(proj)

    proj, d_branch = lax.optimization_barrier((proj, (gate * d_res).astype(bf16)))
    d_branch = gather_rows(d_branch, "seq", seq_down)
    y_fwd, s_row, delta_row = scan_forward(proj, u_low, wdt, bdt, a_two, f32)
    y_col, s_col, delta_col = scan_forward(proj_col, u_col, wdt, bdt, a_two, bf16)
    y_fwd, d_branch = lax.optimization_barrier((y_fwd, d_branch))
    d_branch = d_branch.reshape(total, width)
    u_full = u_low.astype(f32)
    y_all = y_fwd + rows_of(y_col) + dsk * u_full
    silu_z = jax.nn.silu(z_gate)
    gated = (y_all * silu_z).astype(bf16)
    d_gated = dot_t(d_branch, wout)
    d_y = d_gated * silu_z
    d_z = (d_gated * y_all * silu_slope(z_gate)).astype(bf16)
    g_dskip = jnp.sum(d_y * u_full, axis=0)
    rows_each = width // data_parts
    sides = width // chans

    def by_owner(grad):
        return grad.reshape(parts, data_parts, -1, grad.shape[1]).swapaxes(0, 1).reshape(data_parts, rows_each, -1)

    strips = [d_branch[:, k * chans : (k + 1) * chans] for k in range(sides)]
    payload = jnp.concatenate(
        [contract_rows(gated, strip).astype(bf16).reshape(data_parts, -1, chans) for strip in strips]
        + [by_owner(contract_rows(hmod, d_z).astype(bf16))],
        axis=1,
    )
    payload, d_y = lax.optimization_barrier((payload, d_y))
    early = lax.psum_scatter(payload, "dp", scatter_dimension=0, tiled=True)[0]

    dy_col = columns_of(d_y.astype(bf16))
    du_row, p_row, gw_row, gb_row, da_row = scan_adjoint(
        proj, delta_row, u_low, d_y, wdt, a_two, a_low, s_row, f32
    )
    du_col, p_col, gw_col, gb_col, da_col = scan_adjoint(
        proj_col, delta_col, u_col, dy_col, wdt, a_two, a_low, s_col, bf16
    )
    early, p_row, p_col = lax.optimization_barrier((early, p_row, p_col))
    mine = across_seq(early[rows_each:].reshape(parts, -1, chans)).reshape(rows_each, chans)
    mine, p_row, p_col = lax.optimization_barrier((mine, p_row, p_col))
    early = lax.all_gather(jnp.concatenate([early[:rows_each], mine], axis=0), "dp", axis=0)
    p_row, p_col = sum_pair(p_row, p_col)
    d_proj = (p_row + rows_of(p_col.astype(bf16))).astype(bf16)
    g_wx = contract_rows(u_low, d_proj)
    d_u = du_row + rows_of(du_col) + d_y * dsk + dot_t(d_proj, wx)
    d_pre_conv = d_u * silu_slope(pre_conv)
    g_convb = jnp.sum(d_pre_conv, axis=0)
    g_convw = jnp.stack([jnp.sum(padded[k : k + total] * d_pre_conv, axis=0) for k in range(taps)])
    later = jnp.concatenate([d_pre_conv, jnp.zeros((taps - 1, chans), f32)], axis=0)
    d_xconv = sum(cw[:, k] * later[taps - 1 - k : taps - 1 - k + total] for k in range(taps)).astype(bf16)

    half = chans // 2
    singles = [(da_row + da_col) * a_state, gb_row + gb_col, g_dskip[None], g_convb[None], g_convw]
    singles = jnp.concatenate(singles, axis=0).astype(bf16)
    count = singles.shape[0]
    lane = jnp.arange(wdt.shape[1])[None, :]
    singles = contract_rows(singles, (lane == rank + jnp.arange(count)[:, None]).astype(bf16))
    small = jnp.concatenate([g_wx, jnp.where(lane < rank, gw_row + gw_col, singles)], axis=1).astype(bf16)
    columns = small.shape[1]
    if columns <= half:
        small = jnp.pad(small, ((0, 0), (0, half - columns)))
    small = small.reshape(data_parts, -1, half)

    def to_owner(held):
        held = held.astype(bf16)
        mine = across_seq(held[:rows_each].reshape(parts, -1, half)).reshape(rows_each, half)
        return jnp.concatenate([mine, held[rows_each:]], axis=0)

    left = by_owner(contract_rows(hmod, d_xconv[:, :half]).astype(bf16))
    right = by_owner(contract_rows(hmod, d_xconv[:, half:]).astype(bf16))
    right = jnp.concatenate([right, small], axis=1)
    left, right, early = lax.optimization_barrier((left, right, early))
    other_way = dp_up[1:] + dp_up[:1]
    left = scatter_hop(split_bits(left, dp_up), "dp", dp_up, 0)
    right = scatter_hop(split_bits(right, dp_up), "dp", other_way, 0)
    g_out = join_out(early, rows_each, chans)
    g_gate = join_gate(early, rows_each, inner, parts)
    left, right, g_out, g_gate = lax.optimization_barrier((left, right, g_out, g_gate))
    for hop in range(1, len(dp_up)):
        left = scatter_hop(left, "dp", dp_up, hop)
        right = scatter_hop(right, "dp", other_way, hop)
    left = to_owner(left.reshape(rows_each, half))
    right = to_owner(right.reshape(-1, half))
    left = gather_rows(left, "dp", dp_down)
    right = gather_rows(right, "dp", other_way[::-1])
    small = right[:, rows_each:].reshape(-1, half) if columns <= half else right[:, rows_each:].reshape(chans, -1)
    small = small.astype(f32)
    g_in = join_in(g_gate, left, right, parts)

    branch = scatter_sum(dot(gated, wout).astype(bf16).reshape(parts, seq_len, width), "seq", seq_up)
    result = (x_own + gate * branch).astype(bf16)

    d_h = dot_t(d_xconv, w_conv_in) + dot_t(d_z, w_gate_in)
    d_h = scatter_sum(d_h.astype(bf16).reshape(parts, seq_len, width), "seq", seq_up)
    d_x = d_res + norm_back(d_h)[0]

    edges = [0]
    for size in (w_x.shape[1], rank, N, 1, 1, 1, taps):
        edges.append(edges[-1] + size)
    pieces = [small[:, lo:hi] for lo, hi in zip(edges, edges[1:])]
    return (
        result[None],
        d_x[None],
        g_in,
        pieces[0],
        pieces[1],
        pieces[3][:, 0],
        pieces[2],
        pieces[4][:, 0],
        pieces[6],
        pieces[5][:, 0],
        g_out,
    )


def solution(mesh):
    placed = (
        P("dp", "seq", None),
        P("dp", None, None),
        P("dp"),
        P(),
        P(),
        P(),
        P(),
        P(),
        P(),
        P(),
        P(),
        P(),
        P("dp", "seq", None),
    )
    return jax.shard_map(
        shards,
        mesh=mesh,
        in_specs=placed,
        out_specs=(
            P("dp", "seq", None),
            P("dp", "seq", None),
            P("seq", None),
            P("seq", None),
            P("seq", None),
            P("seq"),
            P("seq", None),
            P("seq"),
            P("seq", None),
            P("seq"),
            P("seq", None),
        ),
        check_vma=False,
    )
```
